32 devices in a mesh: groups: 2 (over x), tiles: 16 (over z, y, core).
Axes of the slice: x: 2, y: 2, z: 4, core: 2. Of those that a mesh axis runs over, the one named last changes fastest.
Arguments:
- embeddings: bfloat16 [4096, 4096], P(('groups', 'tiles')), parts along dimension 0, may hold values from -6 to 6
- cluster_tiles: int32 [12], P('groups'), parts along dimension 0, may hold values from 1 to 8, 16 in all
- last_tile_pad: int32 [12], P('groups'), parts along dimension 0, may hold values from 0 to 126
Outputs:
- neighbour_sums: bfloat16 [4096, 4096], P(('groups', 'tiles')), parts along dimension 0
The draws below stay inside these ranges and needn't reach their ends.
There are 2 independent parts, one for each index of `groups`. The reference program is written for one: setup_inputs(seed, part) draws one part's arguments, and reference() takes and returns one part's arrays. A program takes and returns all parts, laid end to end along the dimension named above; each array names one. Nothing has to cross between parts.
Inputs may be any that keep to these rules, and one draw needn't show every extreme that they name: `cluster_tiles`: whole numbers summing to 16; the largest is exactly 8. `last_tile_pad`: every cluster has two or more documents.
All inputs are finite; a program needn't handle non-finite values.
Results may differ from the reference program's by a relative error of at most 0.0085.
Values may be sent and summed in bfloat16 or wider, within the bound.
No kernel may reach another device: no remote copies, remote signals or barrier semaphores. Data moves between devices by JAX's collectives and lax.ppermute only.
A program may use at most 128 MiB of HBM per device.

```python
import math
import jax
import jax.numpy as jnp
import numpy as np
from jax import lax

W = 4096
TILE = 128
MOST = 8
NTILES = 16
ROWS = 2048
NCLUST = 6


def set_ends(drawn, key, smallest, high):
    place = [jax.random.randint(jax.random.fold_in(key, axis), (), 0, length) for axis, length in enumerate(drawn.shape)]
    widest = drawn.shape.index(max(drawn.shape))
    next_to = place[:widest] + [(place[widest] + 1) % drawn.shape[widest]] + place[widest + 1:]
    return drawn.at[tuple(place)].set(smallest).at[tuple(next_to)].set(high)


def level_of(stream_key, dims, shards, least, top_value):
    gain = 1.0
    for axis_at, parts in shards:
        draws = jax.random.uniform(jax.random.fold_in(jax.random.fold_in(stream_key, 6), axis_at), (parts,), jnp.float32, least / len(shards), top_value / len(shards))
        gain = gain * jnp.repeat(jnp.exp(draws), dims[axis_at] // parts).reshape((-1,) + (1,) * (len(dims) - 1 - axis_at))
    return gain


def split_up(amount, total, bound, slope):
    loads = [(1 << 20) // math.isqrt(grade ** slope) + 1 for grade in range(2, amount + 1)]
    surplus, counts = total - bound - (amount - 1), [1] * (amount - 1)
    while surplus > 0:
        candidates = [i for i in range(amount - 1) if counts[i] < bound]
        whole, left = sum([loads[i] for i in candidates]), surplus
        for i in candidates:
            extra = min(bound - counts[i], max(1, left * loads[i] // whole), surplus)
            counts[i] = counts[i] + extra
            surplus = surplus - extra
    return np.array([bound] + counts)


def uneven_parts(rng, number_of, total, limit, lean):
    if number_of == 2:
        one = jax.random.randint(rng, (), max(1, total - limit), min(limit, total - 1) + 1)
        return jnp.stack([one, total - one])
    lengths = jnp.asarray(split_up(number_of, total, limit, lean), jnp.int32)
    twos = (number_of - 1) // 2
    giver, receiver = lengths[1:1 + 2 * twos:2], lengths[2:2 + 2 * twos:2]
    slack = jnp.minimum(giver - 1, limit - receiver)
    passed = jax.random.randint(jax.random.fold_in(rng, 1), (twos,), 0, 1 << 20) % (slack + 1)
    lengths = lengths.at[1:1 + 2 * twos:2].set(giver - passed).at[2:2 + 2 * twos:2].set(receiver + passed)
    return lengths[jax.random.permutation(jax.random.fold_in(rng, 2), number_of)]


def scatter_about(own_key, extent, spread, most, cuts=(), kind=jnp.bfloat16):
    array = spread * jax.random.normal(own_key, extent, jnp.float32)
    if cuts:
        array = array * level_of(own_key, extent, cuts, -0.22, 0.18)
    return jnp.clip(array, -most, most).astype(kind)


def setup_inputs(seed: int = 0, part: int = 0) -> dict:
    key_list = jax.random.split(jax.random.key(seed), 4)
    part_keys = jax.random.split(jax.random.fold_in(key_list[3], part), 4)
    return {
        "embeddings": scatter_about(part_keys[0], (ROWS, W), 1.0, 6.0, ((0, 16),)),
        "cluster_tiles": uneven_parts(part_keys[1], NCLUST, NTILES, MOST, 2).astype(jnp.int32),
        "last_tile_pad": set_ends(jax.random.randint(part_keys[2], (NCLUST,), 0, TILE - 1), jax.random.fold_in(part_keys[2], 1), 0, (TILE - 1) - 1).astype(jnp.int32),
    }


similarity_scale = 64.0

def tile_layout(cluster_tiles, last_tile_pad, tile_index, row_count):
    starts = (jnp.cumsum(cluster_tiles) - cluster_tiles).astype(jnp.int32)
    inside = (starts <= tile_index) & (tile_index < starts + cluster_tiles)
    cluster_ids = jnp.arange(cluster_tiles.shape[0], dtype=jnp.int32)
    present = jnp.any(inside)
    cluster_id = jnp.sum(jnp.where(inside, cluster_ids, 0)).astype(jnp.int32)
    cluster_id = jnp.where(present, cluster_id, -1).astype(jnp.int32)
    cluster_size = cluster_tiles * row_count - last_tile_pad
    live_rows = jnp.sum(jnp.where(inside, cluster_size - (tile_index - starts) * row_count, 0)).astype(jnp.int32)
    live_rows = jnp.clip(live_rows, 0, row_count).astype(jnp.int32)
    return (cluster_id, live_rows)

def inverse_norms(block):
    wide = block.astype(jnp.float32)
    return lax.rsqrt(lax.optimization_barrier(jnp.sum(wide * wide, axis=1)) + 1e-06)

def pair_weights(own_block, inv_own, own_live, other_block, inv_other, other_live, diagonal):
    row_count = own_block.shape[0]
    gram = lax.dot_general(own_block, other_block, (((1,), (1,)), ((), ())), preferred_element_type=jnp.float32)
    row_ids = jnp.arange(row_count, dtype=jnp.int32)
    keep_mask = (row_ids[:, None] < own_live) & (row_ids[None, :] < other_live)
    if diagonal:
        keep_mask = keep_mask & (row_ids[:, None] != row_ids[None, :])
    scores = similarity_scale * inv_own[:, None] * inv_other[None, :] * gram
    return jnp.where(keep_mask, jnp.exp(scores), 0.0).astype(jnp.bfloat16)

def reference(embeddings, cluster_tiles, last_tile_pad):
    tile_stack = embeddings.reshape(NTILES, TILE, W)

    def one_tile(own_index):
        own_block = tile_stack[own_index]
        inv_own = inverse_norms(own_block)
        own_cluster, own_live = tile_layout(cluster_tiles, last_tile_pad, own_index, TILE)
        numer_total = jnp.zeros((TILE, W), jnp.float32)
        denom_total = jnp.zeros((TILE,), jnp.float32)
        for distance in range(-(MOST - 1), MOST):
            other_index = (own_index + distance).astype(jnp.int32)
            clipped = jnp.clip(other_index, 0, NTILES - 1).astype(jnp.int32)
            other_block = tile_stack[clipped]
            other_cluster, other_live = tile_layout(cluster_tiles, last_tile_pad, other_index, TILE)
            same_cluster = (own_cluster == other_cluster) & (other_cluster >= 0)

            def compute_pair(other_block=other_block, other_live=other_live, distance=distance):
                weights = pair_weights(own_block, inv_own, own_live, other_block, inverse_norms(other_block), other_live, distance == 0)
                block_sum = jnp.dot(weights, other_block, preferred_element_type=jnp.float32)
                block_sum = lax.optimization_barrier(block_sum.astype(jnp.bfloat16)).astype(jnp.float32)
                return (block_sum, lax.optimization_barrier(jnp.sum(weights.astype(jnp.float32), axis=1)))

            def skip_pair():
                return (jnp.zeros((TILE, W), jnp.float32), jnp.zeros((TILE,), jnp.float32))
            block_sum, weight_sum = lax.cond(same_cluster, compute_pair, skip_pair)
            numer_total = numer_total + block_sum
            denom_total = denom_total + weight_sum
        live_mask = jnp.arange(TILE, dtype=jnp.int32) < own_live
        safe_denom = jnp.where(live_mask, denom_total, 1.0)
        result = jnp.where(live_mask[:, None], numer_total / safe_denom[:, None], 0.0)
        return result.astype(jnp.bfloat16)
    stacked = lax.map(one_tile, jnp.arange(NTILES, dtype=jnp.int32))
    return stacked.reshape(ROWS, W)
```

```python
import functools

import jax
import jax.numpy as jnp
from jax import lax
from jax.experimental import pallas as pl
from jax.experimental.pallas import tpu as pltpu
from jax.sharding import PartitionSpec as P

MOST = 8
TILE = 128
HALF = 64

similarity_scale = 64.0


def across(row, column, core):
    return row, 1 - column


def along(row, column, core):
    return row + 2 * column - 1, column


def against(row, column, core):
    return row + 1 - 2 * column, column


def far_along(row, column, core):
    return along(row, column, core) if core == column else None


def far_against(row, column, core):
    return against(row, column, core) if core != column else None


STEPS = (
    ("a0", "0", along),
    ("y", "e", across),
    ("b", "e", against),
    ("a1", "1", along),
    ("w0", "a0", across),
    ("w1", "a1", across),
    ("b2", "b", far_against),
    ("x", "y", along),
    ("r0", "w0", against),
    ("r1", "w1", against),
    ("a20", "a0", far_along),
    ("a21", "a1", far_along),
)


def routes(tiles):
    held = {value: [2 * d + (value == "1") for d in range(tiles)] for value in ("0", "1", "e")}
    sizes = {"0": HALF, "1": HALF, "e": TILE}
    pairs, rows, table = [], [], []
    for name, value, direction in STEPS:
        landed, moves = [-1] * tiles, []
        for source in range(tiles):
            target = direction(source // 4, source // 2 % 2, source % 2)
            if target is None or not 0 <= target[0] < tiles // 4 or held[value][source] < 0:
                continue
            place = 4 * target[0] + 2 * target[1] + source % 2
            moves.append((source, place))
            landed[place] = held[value][source]
        held[name], sizes[name] = landed, sizes[value]
        pairs.append(tuple(moves))
        rows.append(sizes[value])
        table.append(landed)
    for device in range(tiles):
        got = []
        for landed, count in zip(table, rows):
            if landed[device] >= 0:
                got += [landed[device]] if count == HALF else [landed[device], landed[device] + 1]
        assert len(got) == len(set(got))
        for tile in (device, device ^ 1):
            for far in range(max(0, tile - MOST + 1), min(tiles, tile + MOST)):
                if far % 2 == device % 2 and far != device:
                    assert {2 * far, 2 * far + 1} <= set(got), (device, far)
    return pairs, rows, table


def attend_kernel(rows, units, clusters, tiles_ref, pad_ref, table_ref, own_ref, sib_ref, *rest):
    pieces = rest[: len(rows)]
    own_out, sib_out, held, weights, limits, den, sems = rest[len(rows) :]
    width = own_ref.shape[1]
    me = lax.axis_index("tiles")
    other = me + 1 - 2 * lax.rem(me, 2)

    def layout(tile):
        start, cluster, live = jnp.int32(0), jnp.int32(-1), jnp.int32(0)
        for c in range(clusters):
            count = tiles_ref[c]
            inside = (start <= tile) & (tile < start + count)
            cluster = jnp.where(inside, c, cluster)
            live = jnp.where(inside, count * TILE - pad_ref[c] - (tile - start) * TILE, live)
            start = start + count
        return cluster, jnp.clip(live, 0, TILE)

    copies = [
        pltpu.make_async_copy(sib_ref, held.at[pl.ds(0, TILE)], sems.at[0]),
        pltpu.make_async_copy(own_ref, held.at[pl.ds(TILE, TILE)], sems.at[1]),
    ]
    for copy in copies:
        copy.start()
    own_cluster, own_live = layout(me)
    sib_cluster, sib_live = layout(other)

    def note(unit, cluster, live):
        limits[0, unit] = jnp.where(cluster == own_cluster, jnp.clip(live, 0, HALF), 0)
        limits[1, unit] = jnp.where(cluster == sib_cluster, jnp.clip(live, 0, HALF), 0)

    note(0, own_cluster, own_live)
    note(1, own_cluster, own_live - HALF)

    used = jnp.int32(2)
    pending = []
    for i, count in enumerate(rows):
        piece = table_ref[me * len(rows) + i]
        cluster, live = layout(lax.shift_right_arithmetic(piece, 1))
        live = live - HALF * (piece & 1)
        valid = (piece >= 0) & ((cluster == own_cluster) | (cluster == sib_cluster))
        place = pl.multiple_of(TILE + used * HALF, HALF)
        copy = pltpu.make_async_copy(pieces[i], held.at[pl.ds(place, count)], sems.at[2 + i])

        @pl.when(valid)
        def _(copy=copy, used=used, cluster=cluster, live=live, count=count):
            copy.start()
            note(used, cluster, live)
            if count == TILE:
                note(used + 1, cluster, live - HALF)

        pending.append((valid, copy))
        used = used + jnp.where(valid, count // HALF, 0)

    few = used <= units // 2
    bound = jnp.where(few, units // 2, units)
    for unit in range(2, units):

        @pl.when((unit >= used) & (unit < bound))
        def _(unit=unit):
            held[pl.ds(TILE + unit * HALF, HALF), :] = jnp.zeros((HALF, width), held.dtype)
            limits[0, unit] = jnp.int32(0)
            limits[1, unit] = jnp.int32(0)

    for copy in copies:
        copy.wait()
    for valid, copy in pending:

        @pl.when(valid)
        def _(copy=copy):
            copy.wait()

    def inverse(block):
        wide = block.astype(jnp.float32)
        return lax.rsqrt(jnp.sum(wide * wide, axis=1, keepdims=True) + 1e-06)

    inv_rows = jnp.concatenate([inverse(held[pl.ds(0, TILE), :]), inverse(held[pl.ds(TILE, TILE), :])], axis=0)
    den[...] = jnp.zeros_like(den)
    row = lax.broadcasted_iota(jnp.int32, (2 * TILE, TILE), 0)
    lane = lax.broadcasted_iota(jnp.int32, (2 * TILE, TILE), 1)
    is_sib = row < TILE
    row_live = row < jnp.where(is_sib, sib_live, own_live + TILE)

    @pl.loop(0, bound // 2)
    def _(b):
        columns = held[pl.ds(pl.multiple_of(TILE + b * TILE, TILE), TILE), :]
        gram = lax.dot_general(
            held[pl.ds(0, 2 * TILE), :], columns, (((1,), (1,)), ((), ())), preferred_element_type=jnp.float32
        )
        inv_columns = jnp.broadcast_to(inverse(columns), (TILE, TILE)).T[0:1, :]
        scores = similarity_scale * inv_rows * inv_columns * gram
        low = jnp.where(is_sib, limits[1, 2 * b], limits[0, 2 * b])
        high = jnp.where(is_sib, limits[1, 2 * b + 1], limits[0, 2 * b + 1])
        keep = row_live & (lane < jnp.where(lane < HALF, low, high + HALF))
        keep = keep & ((row - TILE != lane) | (b != 0))
        block = jnp.where(keep, jnp.exp(scores), 0.0).astype(jnp.bfloat16)
        weights[:, pl.ds(pl.multiple_of(b * TILE, TILE), TILE)] = block
        den[...] += jnp.broadcast_to(jnp.sum(block.astype(jnp.float32), axis=1, keepdims=True), den.shape)

    chunk = 512

    def products(depth):
        @pl.loop(0, width // chunk)
        def _(f):
            at = pl.ds(pl.multiple_of(f * chunk, chunk), chunk)
            total = jnp.dot(
                weights[:, pl.ds(0, depth)], held[pl.ds(TILE, depth), at], preferred_element_type=jnp.float32
            )
            sib_out[:, at] = total[:TILE].astype(jnp.bfloat16)
            own_out[:, at] = total[TILE:]

    @pl.when(few)
    def _():
        products(units // 2 * HALF)

    @pl.when(jnp.logical_not(few))
    def _():
        products(units * HALF)

    own_out[:, pl.ds(width, TILE)] = den[pl.ds(TILE, TILE), :]
    whole = den[pl.ds(0, TILE), :]
    first = whole.astype(jnp.bfloat16).astype(jnp.float32)
    second = (whole - first).astype(jnp.bfloat16).astype(jnp.float32)
    third = whole - first - second
    part = lax.broadcasted_iota(jnp.int32, (TILE, TILE), 1)
    sib_out[:, pl.ds(width, TILE)] = jnp.where(
        part == 0, first, jnp.where(part == 1, second, jnp.where(part == 2, third, 0.0))
    ).astype(jnp.bfloat16)


def attend(tiles, routed, cluster_tiles, last_tile_pad, own, sibling, pieces):
    _, rows, table = routed
    units = 2 * MOST
    width = own.shape[1]
    flat = jnp.array([landed[d] for d in range(tiles) for landed in table], jnp.int32)
    smem = pl.BlockSpec(memory_space=pltpu.SMEM)
    anywhere = pl.BlockSpec(memory_space=pl.ANY)
    vmem = pl.BlockSpec(memory_space=pltpu.VMEM)
    return pl.pallas_call(
        functools.partial(attend_kernel, tuple(rows), units, cluster_tiles.shape[0]),
        out_shape=(
            jax.ShapeDtypeStruct((TILE, width + TILE), jnp.float32),
            jax.ShapeDtypeStruct((TILE, width + TILE), jnp.bfloat16),
        ),
        in_specs=[smem] * 3 + [anywhere] * (2 + len(rows)),
        out_specs=(vmem, vmem),
        scratch_shapes=[
            pltpu.VMEM((TILE + units * HALF, width), jnp.bfloat16),
            pltpu.VMEM((2 * TILE, units * HALF), jnp.bfloat16),
            pltpu.SMEM((2, units), jnp.int32),
            pltpu.VMEM((2 * TILE, TILE), jnp.float32),
            pltpu.SemaphoreType.DMA((2 + len(rows),)),
        ],
        compiler_params=pltpu.CompilerParams(vmem_limit_bytes=32 * 1024 * 1024),
    )(cluster_tiles, last_tile_pad, flat, own, sibling, *pieces)


def body(embeddings, cluster_tiles, last_tile_pad):
    width = embeddings.shape[1]
    tiles = lax.axis_size("tiles")
    routed = routes(tiles)
    cores = [(i, i ^ 1) for i in range(tiles)]
    held = {"0": embeddings[:HALF], "1": embeddings[HALF:], "e": embeddings}
    for (name, value, _), pairs in zip(STEPS, routed[0]):
        held[name] = lax.ppermute(held[value], "tiles", pairs)
    sibling = lax.ppermute(embeddings, "tiles", cores)
    pieces = [held[name] for name, _, _ in STEPS]
    own_sum, sib_sum = attend(tiles, routed, cluster_tiles, last_tile_pad, embeddings, sibling, pieces)
    other_sum = lax.ppermute(sib_sum, "tiles", cores)
    numer = own_sum[:, :width] + other_sum[:, :width].astype(jnp.float32)
    parts = other_sum[:, width : width + 3].astype(jnp.float32)
    denom = own_sum[:, width] + (parts[:, 0] + parts[:, 1] + parts[:, 2])
    live = denom > 0.0
    return jnp.where(live[:, None], numer / jnp.where(live, denom, 1.0)[:, None], 0.0).astype(jnp.bfloat16)


def solution(mesh):
    placed = (P(("groups", "tiles"), None), P("groups"), P("groups"))
    return jax.shard_map(
        body, mesh=mesh, in_specs=placed, out_specs=P(("groups", "tiles"), None), check_vma=False
    )
```

```python
import functools

import jax
import jax.numpy as jnp
from jax import lax
from jax.experimental import pallas as pl
from jax.experimental.pallas import tpu as pltpu
from jax.sharding import PartitionSpec as P

MOST = 8
TILE = 128
HALF = 64

similarity_scale = 64.0


def across(row, column, core):
    return row, 1 - column


def along(row, column, core):
    return row + 2 * column - 1, column


def against(row, column, core):
    return row + 1 - 2 * column, column


def straight(row, column, core):
    return row + 2 * core - 1, column


STEPS = (
    ("a", "e", along),
    ("b", "e", against),
    ("y", "e", across),
    ("w0", ("a", 0), across),
    ("x", "y", along),
    ("w1", ("a", 1), across),
    ("r0", "w0", against),
    ("s", "ab", straight),
    ("r1", "w1", against),
)


def routes(tiles):
    held, sizes = {"e": [2 * d for d in range(tiles)]}, {"e": TILE}
    pairs, rows, table = [], [], []
    for name, value, direction in STEPS:
        if isinstance(value, tuple):
            carried, size = [piece + value[1] if piece >= 0 else -1 for piece in held[value[0]]], HALF
        else:
            carried, size = held[value], sizes[value]
        landed, moves = [-1] * tiles, []
        for source in range(tiles):
            target = direction(source // 4, source // 2 % 2, source % 2)
            if not 0 <= target[0] < tiles // 4 or carried[source] < 0:
                continue
            place = 4 * target[0] + 2 * target[1] + source % 2
            moves.append((source, place))
            landed[place] = carried[source]
        held[name], sizes[name] = landed, size
        if name == "b":
            held["ab"] = [held["a" if d % 2 == d // 2 % 2 else "b"][d] for d in range(tiles)]
            sizes["ab"] = TILE
        pairs.append(tuple(moves))
        rows.append(size)
        table.append(landed)
    for device in range(tiles):
        got = []
        for landed, count in zip(table, rows):
            if landed[device] >= 0:
                got += [landed[device]] if count == HALF else [landed[device], landed[device] + 1]
        assert len(got) == len(set(got))
        for tile in (device, device ^ 1):
            for far in range(max(0, tile - MOST + 1), min(tiles, tile + MOST)):
                if far % 2 == device % 2 and far != device:
                    assert {2 * far, 2 * far + 1} <= set(got), (device, far)
    return pairs, rows, table


def attend_kernel(rows, bounds, clusters, early, tiles_ref, pad_ref, table_ref, *rest):
    own_ref, sib_ref = rest[:2]
    pieces = rest[2 : 2 + len(rows)]
    rest = rest[2 + len(rows) :]
    if not early:
        own_in, sib_in = rest[:2]
        rest = rest[2:]
    own_out, sib_out, held, weights, limits, den, sems = rest
    width = own_ref.shape[1]
    me = lax.axis_index("tiles")
    other = me + 1 - 2 * lax.rem(me, 2)
    base = TILE if early else 2 * TILE

    def layout(tile):
        start, cluster, live = jnp.int32(0), jnp.int32(-1), jnp.int32(0)
        for c in range(clusters):
            count = tiles_ref[c]
            inside = (start <= tile) & (tile < start + count)
            cluster = jnp.where(inside, c, cluster)
            live = jnp.where(inside, count * TILE - pad_ref[c] - (tile - start) * TILE, live)
            start = start + count
        return cluster, jnp.clip(live, 0, TILE)

    copies = [
        pltpu.make_async_copy(sib_ref, held.at[pl.ds(0, TILE)], sems.at[0]),
        pltpu.make_async_copy(own_ref, held.at[pl.ds(TILE, TILE)], sems.at[1]),
    ]
    for copy in copies:
        copy.start()
    own_cluster, own_live = layout(me)
    sib_cluster, sib_live = layout(other)

    def note(unit, cluster, live):
        limits[0, unit] = jnp.where(cluster == own_cluster, jnp.clip(live, 0, HALF), 0)
        limits[1, unit] = jnp.where(cluster == sib_cluster, jnp.clip(live, 0, HALF), 0)

    if early:
        note(0, own_cluster, own_live)
        note(1, own_cluster, own_live - HALF)

    used = jnp.int32(2 if early else 0)
    pending = []
    for i, count in enumerate(rows):
        piece = table_ref[me * len(rows) + i]
        cluster, live = layout(lax.shift_right_arithmetic(piece, 1))
        live = live - HALF * (piece & 1)
        valid = (piece >= 0) & ((cluster == own_cluster) | (cluster == sib_cluster))
        place = pl.multiple_of(base + used * HALF, HALF)
        copy = pltpu.make_async_copy(pieces[i], held.at[pl.ds(place, count)], sems.at[2 + i])

        @pl.when(valid)
        def _(copy=copy, used=used, cluster=cluster, live=live, count=count):
            copy.start()
            note(used, cluster, live)
            if count == TILE:
                note(used + 1, cluster, live - HALF)

        pending.append((valid, copy))
        used = used + jnp.where(valid, count // HALF, 0)

    bound = jnp.int32(bounds[-1])
    for smaller in reversed(bounds[:-1]):
        bound = jnp.where(used <= smaller, smaller, bound)
    for unit in range(2 if early else 0, bounds[-1]):

        @pl.when((unit >= used) & (unit < bound))
        def _(unit=unit):
            held[pl.ds(base + unit * HALF, HALF), :] = jnp.zeros((HALF, width), held.dtype)
            limits[0, unit] = jnp.int32(0)
            limits[1, unit] = jnp.int32(0)

    for copy in copies:
        copy.wait()
    for valid, copy in pending:

        @pl.when(valid)
        def _(copy=copy):
            copy.wait()

    def inverse(at):
        wide = held[at, :].astype(jnp.float32)
        return lax.rsqrt(jnp.sum(wide * wide, axis=1, keepdims=True) + 1e-06)

    wide = 2 * TILE
    if early:
        inv_rows = jnp.concatenate([inverse(pl.ds(0, TILE)), inverse(pl.ds(TILE, TILE))], axis=0)
        sib_out[:, pl.ds(width + TILE, TILE)] = jnp.broadcast_to(inv_rows[:TILE], (TILE, TILE))
        own_out[:, pl.ds(width + TILE, TILE)] = jnp.broadcast_to(inv_rows[TILE:], (TILE, TILE))
        den[...] = jnp.zeros_like(den)
    else:
        at = pl.ds(width + TILE, TILE)
        inv_rows = jnp.concatenate([sib_in[:, at], own_in[:, at]], axis=0)[:, 0:1]
        at = pl.ds(width, TILE)
        den[pl.ds(0, TILE), :] = sib_in[:, at]
        den[pl.ds(TILE, TILE), :] = own_in[:, at]
    row = lax.broadcasted_iota(jnp.int32, (wide, wide), 0)
    lane = lax.broadcasted_iota(jnp.int32, (wide, wide), 1)
    is_sib = row < TILE
    row_live = row < jnp.where(is_sib, sib_live, own_live + TILE)

    @pl.loop(0, bound // 4)
    def _(b):
        start = pl.multiple_of(base + b * wide, TILE)
        gram = lax.dot_general(
            held[pl.ds(0, wide), :],
            held[pl.ds(start, wide), :],
            (((1,), (1,)), ((), ())),
            preferred_element_type=jnp.float32,
        )
        inv_columns = jnp.concatenate(
            [
                jnp.broadcast_to(inverse(pl.ds(pl.multiple_of(start + at, TILE), TILE)), (TILE, TILE)).T[0:1, :]
                for at in (0, TILE)
            ],
            axis=1,
        )
        scores = similarity_scale * inv_rows * inv_columns * gram
        end = jnp.int32(0)
        for u in reversed(range(4)):
            here = u * HALF + jnp.where(is_sib, limits[1, 4 * b + u], limits[0, 4 * b + u])
            end = here if u == 3 else jnp.where(lane < (u + 1) * HALF, here, end)
        keep = row_live & (lane < end)
        if early:
            keep = keep & ((row - TILE != lane) | (b != 0))
        block = jnp.where(keep, jnp.exp(scores), 0.0).astype(jnp.bfloat16)
        weights[:, pl.ds(pl.multiple_of(b * wide, wide), wide)] = block
        den[...] += jnp.broadcast_to(jnp.sum(block.astype(jnp.float32), axis=1, keepdims=True), den.shape)

    chunk = 512

    def products(depth):
        @pl.loop(0, width // chunk)
        def _(f):
            at = pl.ds(pl.multiple_of(f * chunk, chunk), chunk)
            total = jnp.dot(
                weights[:, pl.ds(0, depth)], held[pl.ds(base, depth), at], preferred_element_type=jnp.float32
            )
            if early:
                sib_out[:, at] = total[:TILE]
                own_out[:, at] = total[TILE:]
            else:
                sib_out[:, at] = (sib_in[:, at] + total[:TILE]).astype(jnp.bfloat16)
                own_out[:, at] = own_in[:, at] + total[TILE:]

    for depth in bounds:

        @pl.when(bound == depth)
        def _(depth=depth):
            products(depth * HALF)

    own_out[:, pl.ds(width, TILE)] = den[pl.ds(TILE, TILE), :]
    whole = den[pl.ds(0, TILE), :]
    if early:
        sib_out[:, pl.ds(width, TILE)] = whole
        return
    first = whole.astype(jnp.bfloat16).astype(jnp.float32)
    second = (whole - first).astype(jnp.bfloat16).astype(jnp.float32)
    third = whole - first - second
    part = lax.broadcasted_iota(jnp.int32, (TILE, TILE), 1)
    sib_out[:, pl.ds(width, TILE)] = jnp.where(
        part == 0, first, jnp.where(part == 1, second, jnp.where(part == 2, third, 0.0))
    ).astype(jnp.bfloat16)


def attend(tiles, routed, names, cluster_tiles, last_tile_pad, own, sibling, held, sums=None):
    early = sums is None
    chosen = [i for i, step in enumerate(STEPS) if step[0] in names]
    rows = tuple(routed[1][i] for i in chosen)
    width = own.shape[1]
    flat = jnp.array([routed[2][i][d] for d in range(tiles) for i in chosen], jnp.int32)
    bounds = (4, 8)
    base = TILE if early else 2 * TILE
    assert bounds[-1] * HALF >= sum(rows) + TILE * early
    smem = pl.BlockSpec(memory_space=pltpu.SMEM)
    anywhere = pl.BlockSpec(memory_space=pl.ANY)
    vmem = pl.BlockSpec(memory_space=pltpu.VMEM)
    if early:
        outs = (jax.ShapeDtypeStruct((TILE, width + 2 * TILE), jnp.float32),) * 2
    else:
        outs = tuple(jax.ShapeDtypeStruct((TILE, width + TILE), kind) for kind in (jnp.float32, jnp.bfloat16))
    columns = sum(rows) + TILE * early
    return pl.pallas_call(
        functools.partial(attend_kernel, rows, bounds, cluster_tiles.shape[0], early),
        out_shape=outs,
        in_specs=[smem] * 3 + [anywhere] * (2 + len(rows)) + [vmem] * (0 if early else 2),
        out_specs=(vmem, vmem),
        scratch_shapes=[
            pltpu.VMEM((base + bounds[-1] * HALF, width), jnp.bfloat16),
            pltpu.VMEM((2 * TILE, bounds[-1] * HALF), jnp.bfloat16),
            pltpu.SMEM((2, bounds[-1]), jnp.int32),
            pltpu.VMEM((2 * TILE, TILE), jnp.float32),
            pltpu.SemaphoreType.DMA((2 + len(rows),)),
        ],
        compiler_params=pltpu.CompilerParams(vmem_limit_bytes=32 * 1024 * 1024),
        cost_estimate=pl.CostEstimate(
            flops=8 * TILE * columns * width, bytes_accessed=2 * (columns + 2 * TILE) * width, transcendentals=0
        ),
    )(cluster_tiles, last_tile_pad, flat, own, sibling, *[held[STEPS[i][0]] for i in chosen], *(sums or ()))


FIRST = ("a", "b", "y")


def body(embeddings, cluster_tiles, last_tile_pad):
    width = embeddings.shape[1]
    tiles = lax.axis_size("tiles")
    routed = routes(tiles)
    cores = [(i, i ^ 1) for i in range(tiles)]
    pairs = {step[0]: moves for step, moves in zip(STEPS, routed[0])}
    values = {step[0]: step[1] for step in STEPS}
    held = {"e": embeddings}

    def send(name):
        value = values[name]
        if isinstance(value, tuple):
            operand = held[value[0]][value[1] * HALF : (value[1] + 1) * HALF]
        else:
            operand = held[value]
        held[name] = lax.ppermute(operand, "tiles", pairs[name])

    def together(*names):
        held.update(zip(names, lax.optimization_barrier(tuple(held[name] for name in names))))

    for name in FIRST:
        send(name)
    held["sib"] = lax.ppermute(embeddings, "tiles", cores)
    together("sib", "b", "y", "a")
    send("w0")
    send("x")
    me = lax.axis_index("tiles")
    held["ab"] = jnp.where(me % 2 == me // 2 % 2, held["a"], held["b"])
    send("s")
    together("a", "w0")
    for name in ("r0", "w1", "r1"):
        send(name)
    sibling = held["sib"]
    common = (cluster_tiles, last_tile_pad, embeddings, sibling, held)
    sums = attend(tiles, routed, FIRST, *common)
    rest = [step[0] for step in STEPS if step[0] not in FIRST]
    own_sum, sib_sum = attend(tiles, routed, rest, *common, sums)
    other_sum = lax.ppermute(sib_sum, "tiles", cores)
    numer = own_sum[:, :width] + other_sum[:, :width].astype(jnp.float32)
    parts = other_sum[:, width : width + 3].astype(jnp.float32)
    denom = own_sum[:, width] + (parts[:, 0] + parts[:, 1] + parts[:, 2])
    live = denom > 0.0
    return jnp.where(live[:, None], numer / jnp.where(live, denom, 1.0)[:, None], 0.0).astype(jnp.bfloat16)


def solution(mesh):
    placed = (P(("groups", "tiles"), None), P("groups"), P("groups"))
    return jax.shard_map(
        body, mesh=mesh, in_specs=placed, out_specs=P(("groups", "tiles"), None), check_vma=False
    )
```

```python
import functools

import jax
import jax.numpy as jnp
from jax import lax
from jax.experimental import pallas as pl
from jax.experimental.pallas import tpu as pltpu
from jax.sharding import PartitionSpec as P

MOST = 8
TILE = 128
HALF = 64

similarity_scale = 64.0


def across(row, column, core):
    return row, 1 - column


def along(row, column, core):
    return row + 2 * column - 1, column


def against(row, column, core):
    return row + 1 - 2 * column, column


def straight(row, column, core):
    return row + 2 * core - 1, column


STEPS = (
    ("a", "e", along),
    ("b", "e", against),
    ("y", "e", across),
    ("w0", ("a", 0), across),
    ("x", "y", along),
    ("w1", ("a", 1), across),
    ("r0", "w0", against),
    ("s", "ab", straight),
    ("r1", "w1", against),
)


def routes(tiles):
    held, sizes = {"e": [2 * d for d in range(tiles)]}, {"e": TILE}
    pairs, rows, table = [], [], []
    for name, value, direction in STEPS:
        if isinstance(value, tuple):
            carried, size = [piece + value[1] if piece >= 0 else -1 for piece in held[value[0]]], HALF
        else:
            carried, size = held[value], sizes[value]
        landed, moves = [-1] * tiles, []
        for source in range(tiles):
            target = direction(source // 4, source // 2 % 2, source % 2)
            if not 0 <= target[0] < tiles // 4 or carried[source] < 0:
                continue
            place = 4 * target[0] + 2 * target[1] + source % 2
            moves.append((source, place))
            landed[place] = carried[source]
        held[name], sizes[name] = landed, size
        if name == "b":
            held["ab"] = [held["a" if d % 2 == d // 2 % 2 else "b"][d] for d in range(tiles)]
            sizes["ab"] = TILE
        pairs.append(tuple(moves))
        rows.append(size)
        table.append(landed)
    for device in range(tiles):
        got = []
        for landed, count in zip(table, rows):
            if landed[device] >= 0:
                got += [landed[device]] if count == HALF else [landed[device], landed[device] + 1]
        assert len(got) == len(set(got))
        for tile in (device, device ^ 1):
            for far in range(max(0, tile - MOST + 1), min(tiles, tile + MOST)):
                if far % 2 == device % 2 and far != device:
                    assert {2 * far, 2 * far + 1} <= set(got), (device, far)
    return pairs, rows, table


def attend_kernel(rows, bounds, clusters, early, late, tiles_ref, pad_ref, table_ref, *rest):
    own_ref, sib_ref = rest[:2]
    pieces = rest[2 : 2 + len(rows)]
    rest = rest[2 + len(rows) :]
    if not early:
        own_in, sib_in = rest[:2]
        rest = rest[2:]
    own_out, sib_out, held, weights, limits, den, sems = rest
    width = own_ref.shape[1]
    me = lax.axis_index("tiles")
    other = me + 1 - 2 * lax.rem(me, 2)
    base = TILE if early else 2 * TILE

    def layout(tile):
        start, cluster, live = jnp.int32(0), jnp.int32(-1), jnp.int32(0)
        for c in range(clusters):
            count = tiles_ref[c]
            inside = (start <= tile) & (tile < start + count)
            cluster = jnp.where(inside, c, cluster)
            live = jnp.where(inside, count * TILE - pad_ref[c] - (tile - start) * TILE, live)
            start = start + count
        return cluster, jnp.clip(live, 0, TILE)

    copies = [
        pltpu.make_async_copy(sib_ref, held.at[pl.ds(0, TILE)], sems.at[0]),
        pltpu.make_async_copy(own_ref, held.at[pl.ds(TILE, TILE)], sems.at[1]),
    ]
    for copy in copies:
        copy.start()
    own_cluster, own_live = layout(me)
    sib_cluster, sib_live = layout(other)

    def note(unit, cluster, live):
        limits[0, unit] = jnp.where(cluster == own_cluster, jnp.clip(live, 0, HALF), 0)
        limits[1, unit] = jnp.where(cluster == sib_cluster, jnp.clip(live, 0, HALF), 0)

    if early:
        note(0, own_cluster, own_live)
        note(1, own_cluster, own_live - HALF)

    used = jnp.int32(2 if early else 0)
    pending = []
    for i, count in enumerate(rows):
        piece = table_ref[me * len(rows) + i]
        cluster, live = layout(lax.shift_right_arithmetic(piece, 1))
        live = live - HALF * (piece & 1)
        valid = (piece >= 0) & ((cluster == own_cluster) | (cluster == sib_cluster))
        place = pl.multiple_of(base + used * HALF, HALF)
        copy = pltpu.make_async_copy(pieces[i], held.at[pl.ds(place, count)], sems.at[2 + i])

        @pl.when(valid)
        def _(copy=copy, used=used, cluster=cluster, live=live, count=count):
            copy.start()
            note(used, cluster, live)
            if count == TILE:
                note(used + 1, cluster, live - HALF)

        pending.append((valid, copy))
        used = used + jnp.where(valid, count // HALF, 0)

    bound = jnp.int32(bounds[-1])
    for smaller in reversed(bounds[:-1]):
        bound = jnp.where(used <= smaller, smaller, bound)
    for unit in range(2 if early else 0, bounds[-1]):

        @pl.when((unit >= used) & (unit < bound))
        def _(unit=unit):
            held[pl.ds(base + unit * HALF, HALF), :] = jnp.zeros((HALF, width), held.dtype)
            limits[0, unit] = jnp.int32(0)
            limits[1, unit] = jnp.int32(0)

    for copy in copies:
        copy.wait()
    for valid, copy in pending:

        @pl.when(valid)
        def _(copy=copy):
            copy.wait()

    def inverse(at):
        wide = held[at, :].astype(jnp.float32)
        return lax.rsqrt(jnp.sum(wide * wide, axis=1, keepdims=True) + 1e-06)

    wide = 2 * TILE
    if early:
        inv_rows = jnp.concatenate([inverse(pl.ds(0, TILE)), inverse(pl.ds(TILE, TILE))], axis=0)
        sib_out[:, pl.ds(width + TILE, TILE)] = jnp.broadcast_to(inv_rows[:TILE], (TILE, TILE))
        own_out[:, pl.ds(width + TILE, TILE)] = jnp.broadcast_to(inv_rows[TILE:], (TILE, TILE))
        den[...] = jnp.zeros_like(den)
    else:
        at = pl.ds(width + TILE, TILE)
        inv_rows = jnp.concatenate([sib_in[:, at], own_in[:, at]], axis=0)[:, 0:1]
        if not late:
            sib_out[:, at] = sib_in[:, at]
            own_out[:, at] = own_in[:, at]
        at = pl.ds(width, TILE)
        den[pl.ds(0, TILE), :] = sib_in[:, at]
        den[pl.ds(TILE, TILE), :] = own_in[:, at]
    row = lax.broadcasted_iota(jnp.int32, (wide, wide), 0)
    lane = lax.broadcasted_iota(jnp.int32, (wide, wide), 1)
    is_sib = row < TILE
    row_live = row < jnp.where(is_sib, sib_live, own_live + TILE)

    @pl.loop(0, bound // 4)
    def _(b):
        start = pl.multiple_of(base + b * wide, TILE)
        gram = lax.dot_general(
            held[pl.ds(0, wide), :],
            held[pl.ds(start, wide), :],
            (((1,), (1,)), ((), ())),
            preferred_element_type=jnp.float32,
        )
        inv_columns = jnp.concatenate(
            [
                jnp.broadcast_to(inverse(pl.ds(pl.multiple_of(start + at, TILE), TILE)), (TILE, TILE)).T[0:1, :]
                for at in (0, TILE)
            ],
            axis=1,
        )
        scores = similarity_scale * inv_rows * inv_columns * gram
        end = jnp.int32(0)
        for u in reversed(range(4)):
            here = u * HALF + jnp.where(is_sib, limits[1, 4 * b + u], limits[0, 4 * b + u])
            end = here if u == 3 else jnp.where(lane < (u + 1) * HALF, here, end)
        keep = row_live & (lane < end)
        if early:
            keep = keep & ((row - TILE != lane) | (b != 0))
        block = jnp.where(keep, jnp.exp(scores), 0.0).astype(jnp.bfloat16)
        weights[:, pl.ds(pl.multiple_of(b * wide, wide), wide)] = block
        den[...] += jnp.broadcast_to(jnp.sum(block.astype(jnp.float32), axis=1, keepdims=True), den.shape)

    chunk = 512

    def products(depth):
        @pl.loop(0, width // chunk)
        def _(f):
            at = pl.ds(pl.multiple_of(f * chunk, chunk), chunk)
            total = jnp.dot(
                weights[:, pl.ds(0, depth)], held[pl.ds(base, depth), at], preferred_element_type=jnp.float32
            )
            if early:
                sib_out[:, at] = total[:TILE]
                own_out[:, at] = total[TILE:]
            else:
                sib_out[:, at] = (sib_in[:, at] + total[:TILE]).astype(sib_out.dtype)
                own_out[:, at] = own_in[:, at] + total[TILE:]

    for depth in bounds:

        @pl.when(bound == depth)
        def _(depth=depth):
            products(depth * HALF)

    own_out[:, pl.ds(width, TILE)] = den[pl.ds(TILE, TILE), :]
    whole = den[pl.ds(0, TILE), :]
    if not late:
        sib_out[:, pl.ds(width, TILE)] = whole
        return
    first = whole.astype(jnp.bfloat16).astype(jnp.float32)
    second = (whole - first).astype(jnp.bfloat16).astype(jnp.float32)
    third = whole - first - second
    part = lax.broadcasted_iota(jnp.int32, (TILE, TILE), 1)
    sib_out[:, pl.ds(width, TILE)] = jnp.where(
        part == 0, first, jnp.where(part == 1, second, jnp.where(part == 2, third, 0.0))
    ).astype(jnp.bfloat16)


def attend(tiles, routed, names, cluster_tiles, last_tile_pad, own, sibling, held, sums=None, late=False):
    early = sums is None
    chosen = [i for i, step in enumerate(STEPS) if step[0] in names]
    rows = tuple(routed[1][i] for i in chosen)
    width = own.shape[1]
    flat = jnp.array([routed[2][i][d] for d in range(tiles) for i in chosen], jnp.int32)
    bounds = (4, 8) if early else (4,)
    base = TILE if early else 2 * TILE
    assert bounds[-1] * HALF >= sum(rows) + TILE * early
    smem = pl.BlockSpec(memory_space=pltpu.SMEM)
    anywhere = pl.BlockSpec(memory_space=pl.ANY)
    vmem = pl.BlockSpec(memory_space=pltpu.VMEM)
    if not late:
        outs = (jax.ShapeDtypeStruct((TILE, width + 2 * TILE), jnp.float32),) * 2
    else:
        outs = tuple(jax.ShapeDtypeStruct((TILE, width + TILE), kind) for kind in (jnp.float32, jnp.bfloat16))
    columns = sum(rows) + TILE * early
    return pl.pallas_call(
        functools.partial(attend_kernel, rows, bounds, cluster_tiles.shape[0], early, late),
        out_shape=outs,
        in_specs=[smem] * 3 + [anywhere] * (2 + len(rows)) + [vmem] * (0 if early else 2),
        out_specs=(vmem, vmem),
        scratch_shapes=[
            pltpu.VMEM((base + bounds[-1] * HALF, width), jnp.bfloat16),
            pltpu.VMEM((2 * TILE, bounds[-1] * HALF), jnp.bfloat16),
            pltpu.SMEM((2, bounds[-1]), jnp.int32),
            pltpu.VMEM((2 * TILE, TILE), jnp.float32),
            pltpu.SemaphoreType.DMA((2 + len(rows),)),
        ],
        compiler_params=pltpu.CompilerParams(vmem_limit_bytes=32 * 1024 * 1024),
        cost_estimate=pl.CostEstimate(
            flops=8 * TILE * columns * width, bytes_accessed=2 * (columns + 2 * TILE) * width, transcendentals=0
        ),
    )(cluster_tiles, last_tile_pad, flat, own, sibling, *[held[STEPS[i][0]] for i in chosen], *(sums or ()))


FIRST = ("a", "b", "y")
SECOND = ("w0", "w1", "s")
THIRD = ("x", "r0", "r1")


def body(embeddings, cluster_tiles, last_tile_pad):
    width = embeddings.shape[1]
    tiles = lax.axis_size("tiles")
    routed = routes(tiles)
    cores = [(i, i ^ 1) for i in range(tiles)]
    pairs = {step[0]: moves for step, moves in zip(STEPS, routed[0])}
    values = {step[0]: step[1] for step in STEPS}
    held = {"e": embeddings}

    def send(name):
        value = values[name]
        if isinstance(value, tuple):
            operand = held[value[0]][value[1] * HALF : (value[1] + 1) * HALF]
        else:
            operand = held[value]
        held[name] = lax.ppermute(operand, "tiles", pairs[name])

    def together(*names):
        held.update(zip(names, lax.optimization_barrier(tuple(held[name] for name in names))))

    for name in FIRST:
        send(name)
    held["sib"] = lax.ppermute(embeddings, "tiles", cores)
    together("a", "y")
    send("w0")
    send("x")
    together("sib", "b")
    me = lax.axis_index("tiles")
    held["ab"] = jnp.where(me % 2 == me // 2 % 2, held["a"], held["b"])
    send("s")

    def added(names, **more):
        return attend(
            tiles, routed, names, cluster_tiles, last_tile_pad, embeddings, held["sib"], held, **more
        )

    held["own_sum"], held["sib_sum"] = added(FIRST)
    together("a", "w0", "own_sum", "sib_sum")
    send("w1")
    send("r0")
    together("s", "w1")
    send("r1")
    sums = added(SECOND, sums=(held["own_sum"], held["sib_sum"]))
    own_sum, sib_sum = added(THIRD, sums=sums, late=True)
    other_sum = lax.ppermute(sib_sum, "tiles", cores)
    numer = own_sum[:, :width] + other_sum[:, :width].astype(jnp.float32)
    parts = other_sum[:, width : width + 3].astype(jnp.float32)
    denom = own_sum[:, width] + (parts[:, 0] + parts[:, 1] + parts[:, 2])
    live = denom > 0.0
    return jnp.where(live[:, None], numer / jnp.where(live, denom, 1.0)[:, None], 0.0).astype(jnp.bfloat16)


def solution(mesh):
    placed = (P(("groups", "tiles"), None), P("groups"), P("groups"))
    return jax.shard_map(
        body, mesh=mesh, in_specs=placed, out_specs=P(("groups", "tiles"), None), check_vma=False
    )
```

```python
import functools

import jax
import jax.numpy as jnp
from jax import lax
from jax.experimental import pallas as pl
from jax.experimental.pallas import tpu as pltpu
from jax.sharding import PartitionSpec as P

MOST = 8
TILE = 128
HALF = 64

similarity_scale = 64.0


def across(row, column, core):
    return row, 1 - column


def along(row, column, core):
    return row + 2 * column - 1, column


def against(row, column, core):
    return row + 1 - 2 * column, column


def straight(row, column, core):
    return row + 2 * core - 1, column


STEPS = (
    ("a", "e", along),
    ("b", "e", against),
    ("y", "e", across),
    ("w0", ("a", 0), across),
    ("x", "y", along),
    ("w1", ("a", 1), across),
    ("r0", "w0", against),
    ("s", "ab", straight),
    ("r1", "w1", against),
)


def routes(tiles):
    held, sizes = {"e": [2 * d for d in range(tiles)]}, {"e": TILE}
    pairs, rows, table = [], [], []
    for name, value, direction in STEPS:
        if isinstance(value, tuple):
            carried, size = [piece + value[1] if piece >= 0 else -1 for piece in held[value[0]]], HALF
        else:
            carried, size = held[value], sizes[value]
        landed, moves = [-1] * tiles, []
        for source in range(tiles):
            target = direction(source // 4, source // 2 % 2, source % 2)
            if not 0 <= target[0] < tiles // 4 or carried[source] < 0:
                continue
            place = 4 * target[0] + 2 * target[1] + source % 2
            moves.append((source, place))
            landed[place] = carried[source]
        held[name], sizes[name] = landed, size
        if name == "b":
            held["ab"] = [held["a" if d % 2 == d // 2 % 2 else "b"][d] for d in range(tiles)]
            sizes["ab"] = TILE
        pairs.append(tuple(moves))
        rows.append(size)
        table.append(landed)
    for device in range(tiles):
        got = []
        for landed, count in zip(table, rows):
            if landed[device] >= 0:
                got += [landed[device]] if count == HALF else [landed[device], landed[device] + 1]
        assert len(got) == len(set(got))
        for tile in (device, device ^ 1):
            for far in range(max(0, tile - MOST + 1), min(tiles, tile + MOST)):
                if far % 2 == device % 2 and far != device:
                    assert {2 * far, 2 * far + 1} <= set(got), (device, far)
    return pairs, rows, table


def tile_layout(clusters, tiles_ref, pad_ref, tile):
    start, cluster, live = jnp.int32(0), jnp.int32(-1), jnp.int32(0)
    for c in range(clusters):
        count = tiles_ref[c]
        inside = (start <= tile) & (tile < start + count)
        cluster = jnp.where(inside, c, cluster)
        live = jnp.where(inside, count * TILE - pad_ref[c] - (tile - start) * TILE, live)
        start = start + count
    return cluster, jnp.clip(live, 0, TILE)


def attend_kernel(rows, bounds, clusters, early, late, tiles_ref, pad_ref, table_ref, *rest):
    own_ref, sib_ref = rest[:2]
    pieces = rest[2 : 2 + len(rows)]
    rest = rest[2 + len(rows) :]
    if not early:
        own_in, sib_in = rest[:2]
        rest = rest[2:]
    if late:
        weights_out, rest = rest[0], rest[1:]
    own_out, sib_out, held, weights, limits, den, sems = rest
    width = own_ref.shape[1]
    me = lax.axis_index("tiles")
    other = me + 1 - 2 * lax.rem(me, 2)
    base = TILE if early else 2 * TILE

    layout = functools.partial(tile_layout, clusters, tiles_ref, pad_ref)
    copies = [
        pltpu.make_async_copy(sib_ref, held.at[pl.ds(0, TILE)], sems.at[0]),
        pltpu.make_async_copy(own_ref, held.at[pl.ds(TILE, TILE)], sems.at[1]),
    ]
    for copy in copies:
        copy.start()
    own_cluster, own_live = layout(me)
    sib_cluster, sib_live = layout(other)

    def note(unit, cluster, live):
        limits[0, unit] = jnp.where(cluster == own_cluster, jnp.clip(live, 0, HALF), 0)
        limits[1, unit] = jnp.where(cluster == sib_cluster, jnp.clip(live, 0, HALF), 0)

    if early:
        note(0, own_cluster, own_live)
        note(1, own_cluster, own_live - HALF)

    used = jnp.int32(2 if early else 0)
    pending = []
    for i, count in enumerate(rows):
        piece = table_ref[me * len(rows) + i]
        cluster, live = layout(lax.shift_right_arithmetic(piece, 1))
        live = live - HALF * (piece & 1)
        valid = (piece >= 0) & ((cluster == own_cluster) | (cluster == sib_cluster))
        place = pl.multiple_of(base + used * HALF, HALF)
        copy = pltpu.make_async_copy(pieces[i], held.at[pl.ds(place, count)], sems.at[2 + i])

        @pl.when(valid)
        def _(copy=copy, used=used, cluster=cluster, live=live, count=count):
            copy.start()
            note(used, cluster, live)
            if count == TILE:
                note(used + 1, cluster, live - HALF)

        pending.append((valid, copy))
        used = used + jnp.where(valid, count // HALF, 0)

    bound = jnp.int32(bounds[-1])
    for smaller in reversed(bounds[:-1]):
        bound = jnp.where(used <= smaller, smaller, bound)
    for unit in range(2 if early else 0, bounds[-1]):

        @pl.when((unit >= used) & (unit < bound))
        def _(unit=unit):
            held[pl.ds(base + unit * HALF, HALF), :] = jnp.zeros((HALF, width), held.dtype)
            limits[0, unit] = jnp.int32(0)
            limits[1, unit] = jnp.int32(0)

    for copy in copies:
        copy.wait()
    for valid, copy in pending:

        @pl.when(valid)
        def _(copy=copy):
            copy.wait()

    def inverse(at):
        wide = held[at, :].astype(jnp.float32)
        return lax.rsqrt(jnp.sum(wide * wide, axis=1, keepdims=True) + 1e-06)

    wide = 2 * TILE
    if early:
        inv_rows = jnp.concatenate([inverse(pl.ds(0, TILE)), inverse(pl.ds(TILE, TILE))], axis=0)
        sib_out[:, pl.ds(width + TILE, TILE)] = jnp.broadcast_to(inv_rows[:TILE], (TILE, TILE))
        own_out[:, pl.ds(width + TILE, TILE)] = jnp.broadcast_to(inv_rows[TILE:], (TILE, TILE))
        den[...] = jnp.zeros_like(den)
    else:
        at = pl.ds(width + TILE, TILE)
        inv_rows = jnp.concatenate([sib_in[:, at], own_in[:, at]], axis=0)[:, 0:1]
        if not late:
            sib_out[:, at] = sib_in[:, at]
            own_out[:, at] = own_in[:, at]
        at = pl.ds(width, TILE)
        den[pl.ds(0, TILE), :] = sib_in[:, at]
        den[pl.ds(TILE, TILE), :] = own_in[:, at]
    row = lax.broadcasted_iota(jnp.int32, (wide, wide), 0)
    lane = lax.broadcasted_iota(jnp.int32, (wide, wide), 1)
    is_sib = row < TILE
    row_live = row < jnp.where(is_sib, sib_live, own_live + TILE)

    @pl.loop(0, bound // 4)
    def _(b):
        start = pl.multiple_of(base + b * wide, TILE)
        gram = lax.dot_general(
            held[pl.ds(0, wide), :],
            held[pl.ds(start, wide), :],
            (((1,), (1,)), ((), ())),
            preferred_element_type=jnp.float32,
        )
        inv_columns = jnp.concatenate(
            [
                jnp.broadcast_to(inverse(pl.ds(pl.multiple_of(start + at, TILE), TILE)), (TILE, TILE)).T[0:1, :]
                for at in (0, TILE)
            ],
            axis=1,
        )
        scores = similarity_scale * inv_rows * inv_columns * gram
        end = jnp.int32(0)
        for u in reversed(range(4)):
            here = u * HALF + jnp.where(is_sib, limits[1, 4 * b + u], limits[0, 4 * b + u])
            end = here if u == 3 else jnp.where(lane < (u + 1) * HALF, here, end)
        keep = row_live & (lane < end)
        if early:
            keep = keep & ((row - TILE != lane) | (b != 0))
        block = jnp.where(keep, jnp.exp(scores), 0.0).astype(jnp.bfloat16)
        weights[:, pl.ds(pl.multiple_of(b * wide, wide), wide)] = block
        den[...] += jnp.broadcast_to(jnp.sum(block.astype(jnp.float32), axis=1, keepdims=True), den.shape)

    chunk = 512

    def products(depth):
        @pl.loop(0, width // chunk)
        def _(f):
            at = pl.ds(pl.multiple_of(f * chunk, chunk), chunk)
            total = jnp.dot(
                weights[pl.ds(0, TILE if late else 2 * TILE), pl.ds(0, depth)],
                held[pl.ds(base, depth), at],
                preferred_element_type=jnp.float32,
            )
            if early:
                sib_out[:, at] = total[:TILE]
                own_out[:, at] = total[TILE:]
            else:
                sib_out[:, at] = (sib_in[:, at] + total[:TILE]).astype(sib_out.dtype)
                if not late:
                    own_out[:, at] = own_in[:, at] + total[TILE:]

    for depth in bounds:

        @pl.when(bound == depth)
        def _(depth=depth):
            products(depth * HALF)

    if late:
        weights_out[...] = weights[pl.ds(TILE, TILE), :]
    own_out[:, pl.ds(0 if late else width, TILE)] = den[pl.ds(TILE, TILE), :]
    whole = den[pl.ds(0, TILE), :]
    if not late:
        sib_out[:, pl.ds(width, TILE)] = whole
        return
    first = whole.astype(jnp.bfloat16).astype(jnp.float32)
    second = (whole - first).astype(jnp.bfloat16).astype(jnp.float32)
    third = whole - first - second
    part = lax.broadcasted_iota(jnp.int32, (TILE, TILE), 1)
    sib_out[:, pl.ds(width, TILE)] = jnp.where(
        part == 0, first, jnp.where(part == 1, second, jnp.where(part == 2, third, 0.0))
    ).astype(jnp.bfloat16)


def attend(tiles, routed, names, cluster_tiles, last_tile_pad, own, sibling, held, sums=None, late=False):
    early = sums is None
    chosen = [i for i, step in enumerate(STEPS) if step[0] in names]
    rows = tuple(routed[1][i] for i in chosen)
    width = own.shape[1]
    flat = jnp.array([routed[2][i][d] for d in range(tiles) for i in chosen], jnp.int32)
    bounds = (4, 8) if early else (4,)
    base = TILE if early else 2 * TILE
    assert bounds[-1] * HALF >= sum(rows) + TILE * early
    smem = pl.BlockSpec(memory_space=pltpu.SMEM)
    anywhere = pl.BlockSpec(memory_space=pl.ANY)
    vmem = pl.BlockSpec(memory_space=pltpu.VMEM)
    if not late:
        outs = (jax.ShapeDtypeStruct((TILE, width + 2 * TILE), jnp.float32),) * 2
    else:
        outs = (
            jax.ShapeDtypeStruct((TILE, bounds[-1] * HALF), jnp.bfloat16),
            jax.ShapeDtypeStruct((TILE, TILE), jnp.float32),
            jax.ShapeDtypeStruct((TILE, width + TILE), jnp.bfloat16),
        )
    columns = sum(rows) + TILE * early
    return pl.pallas_call(
        functools.partial(attend_kernel, rows, bounds, cluster_tiles.shape[0], early, late),
        out_shape=outs,
        in_specs=[smem] * 3 + [anywhere] * (2 + len(rows)) + [vmem] * (0 if early else 2),
        out_specs=(vmem,) * len(outs),
        scratch_shapes=[
            pltpu.VMEM((base + bounds[-1] * HALF, width), jnp.bfloat16),
            pltpu.VMEM((2 * TILE, bounds[-1] * HALF), jnp.bfloat16),
            pltpu.SMEM((2, bounds[-1]), jnp.int32),
            pltpu.VMEM((2 * TILE, TILE), jnp.float32),
            pltpu.SemaphoreType.DMA((2 + len(rows),)),
        ],
        compiler_params=pltpu.CompilerParams(vmem_limit_bytes=32 * 1024 * 1024),
        cost_estimate=pl.CostEstimate(
            flops=8 * TILE * columns * width, bytes_accessed=2 * (columns + 2 * TILE) * width, transcendentals=0
        ),
    )(cluster_tiles, last_tile_pad, flat, own, sibling, *[held[STEPS[i][0]] for i in chosen], *(sums or ()))


def own_kernel(rows, units, clusters, tiles_ref, pad_ref, table_ref, *rest):
    pieces = rest[: len(rows)]
    weights_in, own_in, own_out, held, sems = rest[len(rows) :]
    width = own_out.shape[1]
    me = lax.axis_index("tiles")
    layout = functools.partial(tile_layout, clusters, tiles_ref, pad_ref)
    own_cluster, _ = layout(me)
    sib_cluster, _ = layout(me + 1 - 2 * lax.rem(me, 2))
    used = jnp.int32(0)
    pending = []
    for i, count in enumerate(rows):
        piece = table_ref[me * len(rows) + i]
        cluster, _ = layout(lax.shift_right_arithmetic(piece, 1))
        valid = (piece >= 0) & ((cluster == own_cluster) | (cluster == sib_cluster))
        place = pl.multiple_of(used * HALF, HALF)
        copy = pltpu.make_async_copy(pieces[i], held.at[pl.ds(place, count)], sems.at[i])

        @pl.when(valid)
        def _(copy=copy):
            copy.start()

        pending.append((valid, copy))
        used = used + jnp.where(valid, count // HALF, 0)
    for unit in range(units):

        @pl.when(unit >= used)
        def _(unit=unit):
            held[pl.ds(unit * HALF, HALF), :] = jnp.zeros((HALF, width), held.dtype)

    for valid, copy in pending:

        @pl.when(valid)
        def _(copy=copy):
            copy.wait()

    chunk = 512

    @pl.loop(0, width // chunk)
    def _(f):
        at = pl.ds(pl.multiple_of(f * chunk, chunk), chunk)
        own_out[:, at] = own_in[:, at] + jnp.dot(weights_in[...], held[:, at], preferred_element_type=jnp.float32)


def own_products(tiles, routed, names, cluster_tiles, last_tile_pad, held, weights, own_sum):
    chosen = [i for i, step in enumerate(STEPS) if step[0] in names]
    rows = tuple(routed[1][i] for i in chosen)
    depth, width = weights.shape[1], own_sum.shape[1] - 2 * TILE
    flat = jnp.array([routed[2][i][d] for d in range(tiles) for i in chosen], jnp.int32)
    assert sum(rows) <= depth
    smem = pl.BlockSpec(memory_space=pltpu.SMEM)
    vmem = pl.BlockSpec(memory_space=pltpu.VMEM)
    return pl.pallas_call(
        functools.partial(own_kernel, rows, depth // HALF, cluster_tiles.shape[0]),
        out_shape=jax.ShapeDtypeStruct((TILE, width), jnp.float32),
        in_specs=[smem] * 3 + [pl.BlockSpec(memory_space=pl.ANY)] * len(rows) + [vmem] * 2,
        out_specs=vmem,
        scratch_shapes=[
            pltpu.VMEM((depth, width), jnp.bfloat16),
            pltpu.SemaphoreType.DMA((len(rows),)),
        ],
        compiler_params=pltpu.CompilerParams(vmem_limit_bytes=32 * 1024 * 1024),
        cost_estimate=pl.CostEstimate(
            flops=2 * TILE * depth * width, bytes_accessed=2 * depth * width, transcendentals=0
        ),
    )(cluster_tiles, last_tile_pad, flat, *[held[STEPS[i][0]] for i in chosen], weights, own_sum)


FIRST = ("a", "b", "y")
SECOND = ("w0", "w1", "s")
THIRD = ("x", "r0", "r1")


def body(embeddings, cluster_tiles, last_tile_pad):
    width = embeddings.shape[1]
    tiles = lax.axis_size("tiles")
    routed = routes(tiles)
    cores = [(i, i ^ 1) for i in range(tiles)]
    pairs = {step[0]: moves for step, moves in zip(STEPS, routed[0])}
    values = {step[0]: step[1] for step in STEPS}
    held = {"e": embeddings}

    def send(name):
        value = values[name]
        if isinstance(value, tuple):
            operand = held[value[0]][value[1] * HALF : (value[1] + 1) * HALF]
        else:
            operand = held[value]
        held[name] = lax.ppermute(operand, "tiles", pairs[name])

    def together(*names):
        held.update(zip(names, lax.optimization_barrier(tuple(held[name] for name in names))))

    for name in FIRST:
        send(name)
    held["sib"] = lax.ppermute(embeddings, "tiles", cores)
    together("a", "y")
    send("w0")
    send("x")
    together("sib", "b")
    me = lax.axis_index("tiles")
    held["ab"] = jnp.where(me % 2 == me // 2 % 2, held["a"], held["b"])
    send("s")

    def added(names, **more):
        return attend(
            tiles, routed, names, cluster_tiles, last_tile_pad, embeddings, held["sib"], held, **more
        )

    held["own_sum"], held["sib_sum"] = added(FIRST)
    together("a", "w0", "own_sum", "sib_sum")
    send("w1")
    send("r0")
    together("s", "w1")
    send("r1")
    sums = added(SECOND, sums=(held["own_sum"], held["sib_sum"]))
    weights, own_den, sib_sum = added(THIRD, sums=sums, late=True)
    other_sum = lax.ppermute(sib_sum, "tiles", cores)
    own_sum = own_products(tiles, routed, THIRD, cluster_tiles, last_tile_pad, held, weights, sums[0])
    numer = own_sum + other_sum[:, :width].astype(jnp.float32)
    parts = other_sum[:, width : width + 3].astype(jnp.float32)
    denom = own_den[:, 0] + (parts[:, 0] + parts[:, 1] + parts[:, 2])
    live = denom > 0.0
    return jnp.where(live[:, None], numer / jnp.where(live, denom, 1.0)[:, None], 0.0).astype(jnp.bfloat16)


def solution(mesh):
    placed = (P(("groups", "tiles"), None), P("groups"), P("groups"))
    return jax.shard_map(
        body, mesh=mesh, in_specs=placed, out_specs=P(("groups", "tiles"), None), check_vma=False
    )
```

```python
import functools

import jax
import jax.numpy as jnp
from jax import lax
from jax.experimental import pallas as pl
from jax.experimental.pallas import tpu as pltpu
from jax.sharding import PartitionSpec as P

MOST = 8
TILE = 128
HALF = 64

similarity_scale = 64.0


def across(row, column, core):
    return row, 1 - column


def along(row, column, core):
    return row + 2 * column - 1, column


def against(row, column, core):
    return row + 1 - 2 * column, column


def straight(row, column, core):
    return row + 2 * core - 1, column


STEPS = (
    ("a", "e", along),
    ("b", "e", against),
    ("y", "e", across),
    ("w0", ("a", 0), across),
    ("x", "y", along),
    ("w1", ("a", 1), across),
    ("r0", "w0", against),
    ("s", "ab", straight),
    ("r1", "w1", against),
)


def routes(tiles):
    held, sizes = {"e": [2 * d for d in range(tiles)]}, {"e": TILE}
    pairs, rows, table = [], [], []
    for name, value, direction in STEPS:
        if isinstance(value, tuple):
            carried, size = [piece + value[1] if piece >= 0 else -1 for piece in held[value[0]]], HALF
        else:
            carried, size = held[value], sizes[value]
        landed, moves = [-1] * tiles, []
        for source in range(tiles):
            target = direction(source // 4, source // 2 % 2, source % 2)
            if not 0 <= target[0] < tiles // 4 or carried[source] < 0:
                continue
            place = 4 * target[0] + 2 * target[1] + source % 2
            moves.append((source, place))
            landed[place] = carried[source]
        held[name], sizes[name] = landed, size
        if name == "b":
            held["ab"] = [held["a" if d % 2 == d // 2 % 2 else "b"][d] for d in range(tiles)]
            sizes["ab"] = TILE
        pairs.append(tuple(moves))
        rows.append(size)
        table.append(landed)
    for device in range(tiles):
        got = []
        for landed, count in zip(table, rows):
            if landed[device] >= 0:
                got += [landed[device]] if count == HALF else [landed[device], landed[device] + 1]
        assert len(got) == len(set(got))
        for tile in (device, device ^ 1):
            for far in range(max(0, tile - MOST + 1), min(tiles, tile + MOST)):
                if far % 2 == device % 2 and far != device:
                    assert {2 * far, 2 * far + 1} <= set(got), (device, far)
    return pairs, rows, table


def tile_layout(clusters, tiles_ref, pad_ref, tile):
    start, cluster, live = jnp.int32(0), jnp.int32(-1), jnp.int32(0)
    for c in range(clusters):
        count = tiles_ref[c]
        inside = (start <= tile) & (tile < start + count)
        cluster = jnp.where(inside, c, cluster)
        live = jnp.where(inside, count * TILE - pad_ref[c] - (tile - start) * TILE, live)
        start = start + count
    return cluster, jnp.clip(live, 0, TILE)


def attend_kernel(rows, bounds, clusters, early, late, tiles_ref, pad_ref, table_ref, *rest):
    own_ref, sib_ref = rest[:2]
    pieces = rest[2 : 2 + len(rows)]
    rest = rest[2 + len(rows) :]
    if not early:
        own_in, sib_in = rest[:2]
        rest = rest[2:]
    if late:
        weights_out, rest = rest[0], rest[1:]
    own_out, sib_out, held, weights, limits, den, sems = rest
    width = own_ref.shape[1]
    me = lax.axis_index("tiles")
    other = me + 1 - 2 * lax.rem(me, 2)
    base = TILE if early else 2 * TILE

    layout = functools.partial(tile_layout, clusters, tiles_ref, pad_ref)
    copies = [
        pltpu.make_async_copy(sib_ref, held.at[pl.ds(0, TILE)], sems.at[0]),
        pltpu.make_async_copy(own_ref, held.at[pl.ds(TILE, TILE)], sems.at[1]),
    ]
    for copy in copies:
        copy.start()
    own_cluster, own_live = layout(me)
    sib_cluster, sib_live = layout(other)

    def note(unit, cluster, live):
        limits[0, unit] = jnp.where(cluster == own_cluster, jnp.clip(live, 0, HALF), 0)
        limits[1, unit] = jnp.where(cluster == sib_cluster, jnp.clip(live, 0, HALF), 0)

    if early:
        note(0, own_cluster, own_live)
        note(1, own_cluster, own_live - HALF)

    used = jnp.int32(2 if early else 0)
    pending = []
    for i, count in enumerate(rows):
        piece = table_ref[me * len(rows) + i]
        cluster, live = layout(lax.shift_right_arithmetic(piece, 1))
        live = live - HALF * (piece & 1)
        valid = (piece >= 0) & ((cluster == own_cluster) | (cluster == sib_cluster))
        place = pl.multiple_of(base + used * HALF, HALF)
        copy = pltpu.make_async_copy(pieces[i], held.at[pl.ds(place, count)], sems.at[2 + i])

        @pl.when(valid)
        def _(copy=copy, used=used, cluster=cluster, live=live, count=count):
            copy.start()
            note(used, cluster, live)
            if count == TILE:
                note(used + 1, cluster, live - HALF)

        pending.append((valid, copy))
        used = used + jnp.where(valid, count // HALF, 0)

    bound = jnp.int32(bounds[-1])
    for smaller in reversed(bounds[:-1]):
        bound = jnp.where(used <= smaller, smaller, bound)
    for unit in range(2 if early else 0, bounds[-1]):

        @pl.when((unit >= used) & (unit < bound))
        def _(unit=unit):
            held[pl.ds(base + unit * HALF, HALF), :] = jnp.zeros((HALF, width), held.dtype)
            limits[0, unit] = jnp.int32(0)
            limits[1, unit] = jnp.int32(0)

    for copy in copies:
        copy.wait()
    for valid, copy in pending:

        @pl.when(valid)
        def _(copy=copy):
            copy.wait()

    def inverse(at):
        wide = held[at, :].astype(jnp.float32)
        return lax.rsqrt(jnp.sum(wide * wide, axis=1, keepdims=True) + 1e-06)

    wide = 2 * TILE
    if early:
        inv_rows = jnp.concatenate([inverse(pl.ds(0, TILE)), inverse(pl.ds(TILE, TILE))], axis=0)
        sib_out[:, pl.ds(width + TILE, TILE)] = jnp.broadcast_to(inv_rows[:TILE], (TILE, TILE))
        own_out[:, pl.ds(width + TILE, TILE)] = jnp.broadcast_to(inv_rows[TILE:], (TILE, TILE))
        den[...] = jnp.zeros_like(den)
    else:
        at = pl.ds(width + TILE, TILE)
        inv_rows = jnp.concatenate([sib_in[:, at], own_in[:, at]], axis=0)[:, 0:1]
        if not late:
            sib_out[:, at] = sib_in[:, at]
            own_out[:, at] = own_in[:, at]
        at = pl.ds(width, TILE)
        den[pl.ds(0, TILE), :] = sib_in[:, at]
        den[pl.ds(TILE, TILE), :] = own_in[:, at]
    row = lax.broadcasted_iota(jnp.int32, (wide, wide), 0)
    lane = lax.broadcasted_iota(jnp.int32, (wide, wide), 1)
    is_sib = row < TILE
    row_live = row < jnp.where(is_sib, sib_live, own_live + TILE)

    @pl.loop(0, bound // 4)
    def _(b):
        start = pl.multiple_of(base + b * wide, TILE)
        gram = lax.dot_general(
            held[pl.ds(0, wide), :],
            held[pl.ds(start, wide), :],
            (((1,), (1,)), ((), ())),
            preferred_element_type=jnp.float32,
        )
        inv_columns = jnp.concatenate(
            [
                jnp.broadcast_to(inverse(pl.ds(pl.multiple_of(start + at, TILE), TILE)), (TILE, TILE)).T[0:1, :]
                for at in (0, TILE)
            ],
            axis=1,
        )
        scores = similarity_scale * inv_rows * inv_columns * gram
        end = jnp.int32(0)
        for u in reversed(range(4)):
            here = u * HALF + jnp.where(is_sib, limits[1, 4 * b + u], limits[0, 4 * b + u])
            end = here if u == 3 else jnp.where(lane < (u + 1) * HALF, here, end)
        keep = row_live & (lane < end)
        if early:
            keep = keep & ((row - TILE != lane) | (b != 0))
        block = jnp.where(keep, jnp.exp(scores), 0.0).astype(jnp.bfloat16)
        weights[:, pl.ds(pl.multiple_of(b * wide, wide), wide)] = block
        den[...] += jnp.broadcast_to(jnp.sum(block.astype(jnp.float32), axis=1, keepdims=True), den.shape)

    chunk = 1024

    def products(depth):
        @pl.loop(0, width // chunk)
        def _(f):
            at = pl.ds(pl.multiple_of(f * chunk, chunk), chunk)
            total = jnp.dot(
                weights[pl.ds(0, TILE if late else 2 * TILE), pl.ds(0, depth)],
                held[pl.ds(base, depth), at],
                preferred_element_type=jnp.float32,
            )
            if early:
                sib_out[:, at] = total[:TILE]
                own_out[:, at] = total[TILE:]
            else:
                sib_out[:, at] = (sib_in[:, at] + total[:TILE]).astype(sib_out.dtype)
                if not late:
                    own_out[:, at] = own_in[:, at] + total[TILE:]

    for depth in bounds:

        @pl.when(bound == depth)
        def _(depth=depth):
            products(depth * HALF)

    if late:
        weights_out[...] = weights[pl.ds(TILE, TILE), :]
    own_out[:, pl.ds(0 if late else width, TILE)] = den[pl.ds(TILE, TILE), :]
    whole = den[pl.ds(0, TILE), :]
    if not late:
        sib_out[:, pl.ds(width, TILE)] = whole
        return
    first = whole.astype(jnp.bfloat16).astype(jnp.float32)
    second = (whole - first).astype(jnp.bfloat16).astype(jnp.float32)
    third = whole - first - second
    part = lax.broadcasted_iota(jnp.int32, (TILE, TILE), 1)
    sib_out[:, pl.ds(width, TILE)] = jnp.where(
        part == 0, first, jnp.where(part == 1, second, jnp.where(part == 2, third, 0.0))
    ).astype(jnp.bfloat16)


def attend(tiles, routed, names, cluster_tiles, last_tile_pad, own, sibling, held, sums=None, late=False):
    early = sums is None
    chosen = [i for i, step in enumerate(STEPS) if step[0] in names]
    rows = tuple(routed[1][i] for i in chosen)
    width = own.shape[1]
    flat = jnp.array([routed[2][i][d] for d in range(tiles) for i in chosen], jnp.int32)
    bounds = (4, 8) if early else (4,)
    base = TILE if early else 2 * TILE
    assert bounds[-1] * HALF >= sum(rows) + TILE * early
    smem = pl.BlockSpec(memory_space=pltpu.SMEM)
    anywhere = pl.BlockSpec(memory_space=pl.ANY)
    vmem = pl.BlockSpec(memory_space=pltpu.VMEM)
    if not late:
        outs = (jax.ShapeDtypeStruct((TILE, width + 2 * TILE), jnp.float32),) * 2
    else:
        outs = (
            jax.ShapeDtypeStruct((TILE, bounds[-1] * HALF), jnp.bfloat16),
            jax.ShapeDtypeStruct((TILE, TILE), jnp.float32),
            jax.ShapeDtypeStruct((TILE, width + TILE), jnp.bfloat16),
        )
    columns = sum(rows) + TILE * early
    return pl.pallas_call(
        functools.partial(attend_kernel, rows, bounds, cluster_tiles.shape[0], early, late),
        out_shape=outs,
        in_specs=[smem] * 3 + [anywhere] * (2 + len(rows)) + [vmem] * (0 if early else 2),
        out_specs=(vmem,) * len(outs),
        scratch_shapes=[
            pltpu.VMEM((base + bounds[-1] * HALF, width), jnp.bfloat16),
            pltpu.VMEM((2 * TILE, bounds[-1] * HALF), jnp.bfloat16),
            pltpu.SMEM((2, bounds[-1]), jnp.int32),
            pltpu.VMEM((2 * TILE, TILE), jnp.float32),
            pltpu.SemaphoreType.DMA((2 + len(rows),)),
        ],
        compiler_params=pltpu.CompilerParams(vmem_limit_bytes=32 * 1024 * 1024),
        cost_estimate=pl.CostEstimate(
            flops=8 * TILE * columns * width, bytes_accessed=2 * (columns + 2 * TILE) * width, transcendentals=0
        ),
    )(cluster_tiles, last_tile_pad, flat, own, sibling, *[held[STEPS[i][0]] for i in chosen], *(sums or ()))


def own_kernel(rows, units, clusters, tiles_ref, pad_ref, table_ref, *rest):
    pieces = rest[: len(rows)]
    weights_in, own_in, own_out, held, sems = rest[len(rows) :]
    width = own_out.shape[1]
    me = lax.axis_index("tiles")
    layout = functools.partial(tile_layout, clusters, tiles_ref, pad_ref)
    own_cluster, _ = layout(me)
    sib_cluster, _ = layout(me + 1 - 2 * lax.rem(me, 2))
    used = jnp.int32(0)
    pending = []
    for i, count in enumerate(rows):
        piece = table_ref[me * len(rows) + i]
        cluster, _ = layout(lax.shift_right_arithmetic(piece, 1))
        valid = (piece >= 0) & ((cluster == own_cluster) | (cluster == sib_cluster))
        place = pl.multiple_of(used * HALF, HALF)
        copy = pltpu.make_async_copy(pieces[i], held.at[pl.ds(place, count)], sems.at[i])

        @pl.when(valid)
        def _(copy=copy):
            copy.start()

        pending.append((valid, copy))
        used = used + jnp.where(valid, count // HALF, 0)
    for unit in range(units):

        @pl.when(unit >= used)
        def _(unit=unit):
            held[pl.ds(unit * HALF, HALF), :] = jnp.zeros((HALF, width), held.dtype)

    for valid, copy in pending:

        @pl.when(valid)
        def _(copy=copy):
            copy.wait()

    chunk = 1024

    @pl.loop(0, width // chunk)
    def _(f):
        at = pl.ds(pl.multiple_of(f * chunk, chunk), chunk)
        own_out[:, at] = own_in[:, at] + jnp.dot(weights_in[...], held[:, at], preferred_element_type=jnp.float32)


def own_products(tiles, routed, names, cluster_tiles, last_tile_pad, held, weights, own_sum):
    chosen = [i for i, step in enumerate(STEPS) if step[0] in names]
    rows = tuple(routed[1][i] for i in chosen)
    depth, width = weights.shape[1], own_sum.shape[1] - 2 * TILE
    flat = jnp.array([routed[2][i][d] for d in range(tiles) for i in chosen], jnp.int32)
    assert sum(rows) <= depth
    smem = pl.BlockSpec(memory_space=pltpu.SMEM)
    vmem = pl.BlockSpec(memory_space=pltpu.VMEM)
    return pl.pallas_call(
        functools.partial(own_kernel, rows, depth // HALF, cluster_tiles.shape[0]),
        out_shape=jax.ShapeDtypeStruct((TILE, width), jnp.float32),
        in_specs=[smem] * 3 + [pl.BlockSpec(memory_space=pl.ANY)] * len(rows) + [vmem] * 2,
        out_specs=vmem,
        scratch_shapes=[
            pltpu.VMEM((depth, width), jnp.bfloat16),
            pltpu.SemaphoreType.DMA((len(rows),)),
        ],
        compiler_params=pltpu.CompilerParams(vmem_limit_bytes=32 * 1024 * 1024),
        cost_estimate=pl.CostEstimate(
            flops=2 * TILE * depth * width, bytes_accessed=2 * depth * width, transcendentals=0
        ),
    )(cluster_tiles, last_tile_pad, flat, *[held[STEPS[i][0]] for i in chosen], weights, own_sum)


FIRST = ("a", "b", "y")
SECOND = ("w0", "w1", "s")
THIRD = ("x", "r0", "r1")


def body(embeddings, cluster_tiles, last_tile_pad):
    width = embeddings.shape[1]
    tiles = lax.axis_size("tiles")
    routed = routes(tiles)
    cores = [(i, i ^ 1) for i in range(tiles)]
    pairs = {step[0]: moves for step, moves in zip(STEPS, routed[0])}
    values = {step[0]: step[1] for step in STEPS}
    held = {"e": embeddings}

    def send(name):
        value = values[name]
        if isinstance(value, tuple):
            operand = held[value[0]][value[1] * HALF : (value[1] + 1) * HALF]
        else:
            operand = held[value]
        held[name] = lax.ppermute(operand, "tiles", pairs[name])

    def together(*names):
        held.update(zip(names, lax.optimization_barrier(tuple(held[name] for name in names))))

    for name in FIRST:
        send(name)
    held["sib"] = lax.ppermute(embeddings, "tiles", cores)
    together("a", "y")
    send("w0")
    send("x")
    together("sib", "b")
    me = lax.axis_index("tiles")
    held["ab"] = jnp.where(me % 2 == me // 2 % 2, held["a"], held["b"])
    send("s")

    def added(names, **more):
        return attend(
            tiles, routed, names, cluster_tiles, last_tile_pad, embeddings, held["sib"], held, **more
        )

    held["own_sum"], held["sib_sum"] = added(FIRST)
    together("a", "w0", "own_sum", "sib_sum")
    send("w1")
    send("r0")
    together("s", "w1")
    send("r1")
    sums = added(SECOND, sums=(held["own_sum"], held["sib_sum"]))
    weights, own_den, sib_sum = added(THIRD, sums=sums, late=True)
    other_sum = lax.ppermute(sib_sum, "tiles", cores)
    own_sum = own_products(tiles, routed, THIRD, cluster_tiles, last_tile_pad, held, weights, sums[0])
    numer = own_sum + other_sum[:, :width].astype(jnp.float32)
    parts = other_sum[:, width : width + 3].astype(jnp.float32)
    denom = own_den[:, 0] + (parts[:, 0] + parts[:, 1] + parts[:, 2])
    live = denom > 0.0
    return jnp.where(live[:, None], numer / jnp.where(live, denom, 1.0)[:, None], 0.0).astype(jnp.bfloat16)


def solution(mesh):
    placed = (P(("groups", "tiles"), None), P("groups"), P("groups"))
    return jax.shard_map(
        body, mesh=mesh, in_specs=placed, out_specs=P(("groups", "tiles"), None), check_vma=False
    )
```
